256 devices in a mesh: item: 32 (over x_hi, z, core), sub: 8 (over x_lo, y).
Axes of the slice: x: 4 (x_hi: 2, x_lo: 2; x = x_hi * 2 + x_lo), y: 4, z: 8, core: 2. Of those that a mesh axis runs over, the one named last changes fastest.
Arguments:
- samples: bfloat16 [65536, 1024], P(('item', 'sub')), may hold values from -28 to 28
- rotation: bfloat16 [1024, 1024], replicated, may hold values from -0.1875 to 0.1875
- codebook: bfloat16 [8, 4096, 128], P('sub'), may hold values from -4 to 4
Outputs:
- codewords_new: float32 [8, 4096, 128], P('sub', 'item')
- cross_cov: float32 [1024, 1024], P('item', 'sub')
The draws below stay inside these ranges and needn't reach their ends.
All inputs are finite; a program needn't handle non-finite values.
Results may differ from the reference program's by a relative error of at most 0.011.
Values may be sent and summed in bfloat16 or wider, within the bound.
A program may use at most 64 MiB of HBM per device.

```python
import math
import jax
import jax.numpy as jnp
from jax import lax

D = 1024
S = 128
K = 4096
M = 8
ROWS = 65536


def draw_samples(key, part):
    key = jax.random.fold_in(key, 1)
    key_scale, key_value = jax.random.split(key)
    scales = jnp.exp(jax.random.uniform(key_scale, (ROWS, 1), jnp.float32, math.log(0.7), math.log(1.4)))
    values = jnp.clip(jax.random.normal(key_value, (ROWS, D), jnp.float32), -4.0, 4.0)
    return (values * scales).astype(jnp.bfloat16)


def level_of(own_key, extent, cuts, smallest, largest):
    level = 1.0
    for position, parts in cuts:
        draws = jax.random.uniform(jax.random.fold_in(jax.random.fold_in(own_key, 6), position), (parts,), jnp.float32, smallest / len(cuts), largest / len(cuts))
        level = level * jnp.repeat(jnp.exp(draws), extent[position] // parts).reshape((-1,) + (1,) * (len(extent) - 1 - position))
    return level


def centred(key, dims, deviation, bound, pieces=(), dtype=jnp.bfloat16):
    drawn = deviation * jax.random.normal(key, dims, jnp.float32)
    if pieces:
        drawn = drawn * level_of(key, dims, pieces, -0.22, 0.18)
    return jnp.clip(drawn, -bound, bound).astype(dtype)


def setup_inputs(seed: int = 0) -> dict:
    streams_of = jax.random.split(jax.random.key(seed), 4)
    return {
        "samples": draw_samples(jax.random.fold_in(streams_of[3], 71), 0),
        "rotation": centred(streams_of[1], (D, D), D ** -0.5, 0.1875),
        "codebook": centred(streams_of[2], (M, K, S), 1.0, 4.0, ((0, 8),)),
    }


def assign_subspace(rotated_sub, codewords):
    code_f = codewords.astype(jnp.float32)
    sqnorm = lax.optimization_barrier(jnp.sum(code_f * code_f, axis=1))
    sharpness = 3.0 / math.sqrt(S)
    total_rows = rotated_sub.shape[0]
    block_rows = math.gcd(total_rows, 2048)
    blocks = rotated_sub.reshape(total_rows // block_rows, block_rows, S)

    def step(carry, block):
        counts, totals = carry
        logits = (jnp.dot(block, codewords.T, preferred_element_type=jnp.float32) - 0.5 * sqnorm[None, :]) * sharpness
        weights = jax.nn.softmax(logits, axis=1).astype(jnp.bfloat16)
        counts = counts + lax.optimization_barrier(jnp.sum(weights.astype(jnp.float32), axis=0))
        totals = totals + jnp.dot(weights.T, block, preferred_element_type=jnp.float32)
        rebuilt = jnp.dot(weights, codewords, preferred_element_type=jnp.float32).astype(jnp.bfloat16)
        return ((counts, totals), rebuilt)
    init = (jnp.zeros((K,), jnp.float32), jnp.zeros((K, S), jnp.float32))
    (counts, totals), rebuilt = lax.scan(step, init, blocks)
    fresh = (totals + code_f) / (counts + 1.0)[:, None]
    return (fresh, rebuilt.reshape(total_rows, S))

def reference(samples, rotation, codebook):
    rotated = jnp.dot(samples, rotation, preferred_element_type=jnp.float32).astype(jnp.bfloat16)
    fresh_list = []
    rebuilt_list = []
    for member in range(M):
        fresh, rebuilt = assign_subspace(rotated[:, member * S:(member + 1) * S], codebook[member])
        fresh_list.append(fresh)
        rebuilt_list.append(rebuilt)
    codewords_new = jnp.stack(fresh_list, axis=0)
    rebuilt_all = jnp.concatenate(rebuilt_list, axis=1)
    cross_cov = jnp.dot(samples.T, rebuilt_all, preferred_element_type=jnp.float32)
    return (codewords_new, cross_cov)
```

```python
import math

import jax
import jax.numpy as jnp
from jax import lax
from jax.experimental import pallas as pl
from jax.experimental.pallas import tpu as pltpu
from jax.sharding import PartitionSpec as P

BF = jnp.bfloat16
F32 = jnp.float32
MESH = pl.DeviceIdType.MESH
NT = (((1,), (1,)), ((), ()))

D, S, K, ROWS, SUBS, CHIPS = 1024, 128, 4096, 256, 8, 16
KC = 512
TC = 512
EXT = S + 16
SCALE = 3.0 / math.sqrt(S) * math.log2(math.e)


def kernel(
    samples_hbm, rotation_hbm, codebook_hbm,
    fresh_ref, cross_ref,
    samples, rotation, codes, codes_aug, codes_ext,
    sam_t, sam_sib,
    z_send, z_recv, zl, logits_a, logits_b, weights,
    reb_send, reb_recv, reb_sib,
    cov_own, cov_send, cov_recv, cov2_own, cov2_send, cov2_recv,
    tot_f, tot_b, tot_sib, tot_own, tot_send, tot_recv,
    load_sem, z_ss, z_rs, r_ss, r_rs, f_ss, f_rs, s_ss, s_rs,
    c_ss, c_rs, c2_ss, c2_rs, ts_ss, ts_rs, t_ss, t_rs,
):
    item, sub = lax.axis_index("item"), lax.axis_index("sub")
    core, chip = item % 2, item // 2
    sibling = item + 1 - 2 * core
    xl, y = sub // 4, sub % 4

    loads = [
        pltpu.make_async_copy(samples_hbm, samples, load_sem.at[0]),
        pltpu.make_async_copy(rotation_hbm, rotation, load_sem.at[1]),
        pltpu.make_async_copy(codebook_hbm.at[0], codes, load_sem.at[2]),
    ]
    for load in loads:
        load.start()

    barrier = pltpu.get_barrier_semaphore()

    def greet(i, s):
        pl.semaphore_signal(barrier, inc=1, device_id={"item": i, "sub": s}, device_id_type=MESH)

    def greet_sub(j, carry):
        greet(item, (sub + j) % SUBS)
        return carry

    def greet_chip(j, carry):
        greet((chip + j) % CHIPS * 2 + core, sub)
        return carry

    lax.fori_loop(1, SUBS, greet_sub, 0)
    lax.fori_loop(1, CHIPS, greet_chip, 0)
    greet(sibling, sub)

    def remote(src, dst, ss, rs, i, s):
        return pltpu.make_async_remote_copy(
            src_ref=src, dst_ref=dst, send_sem=ss, recv_sem=rs,
            device_id={"item": i, "sub": s}, device_id_type=MESH,
        )

    def z_copy(dest, src):
        return remote(z_send.at[dest], z_recv.at[src], z_ss.at[dest], z_rs.at[src], item, dest)

    def r_copy(dest, src):
        return remote(reb_send.at[dest], reb_recv.at[src], r_ss.at[dest], r_rs.at[src], item, dest)

    def f_copy(m):
        return remote(reb_recv.at[m], reb_sib.at[m], f_ss.at[m], f_rs.at[m], sibling, sub)

    def s_copy():
        return remote(sam_t.at[1 - core], sam_sib, s_ss, s_rs, sibling, sub)

    def c_copy(dest, src):
        return remote(cov_send.at[dest], cov_recv.at[src], c_ss.at[dest], c_rs.at[src], item, dest)

    def c2_copy(dest, src):
        return remote(
            cov2_send.at[dest], cov2_recv.at[src], c2_ss.at[dest], c2_rs.at[src], dest * 2 + core, sub
        )

    def ts_copy(g):
        return remote(tot_b.at[g, 1 - core], tot_sib.at[g], ts_ss.at[g], ts_rs.at[g], sibling, sub)

    def t_copy(dest, src):
        return remote(
            tot_send.at[dest], tot_recv.at[src], t_ss.at[dest], t_rs.at[src], dest * 2 + core, sub
        )

    def owner(t):
        return (xl + t // 4) % 2 * 4 + (y + t) % 4

    def origin(t):
        return (xl + t // 4) % 2 * 4 + (y + 8 - t) % 4

    loads[0].wait()
    loads[1].wait()
    pl.semaphore_wait(barrier, SUBS - 1 + CHIPS - 1 + 1)

    for step in range(4):
        pair = (sub // 2 + step) % 4
        rotated = jnp.dot(
            samples[...], rotation[:, pl.ds(pl.multiple_of(pair * 256, 256), 256)],
            preferred_element_type=F32,
        )
        rotated_t = rotated.T.astype(BF)
        for half in range(2):
            m = pair * 2 + half
            z_send[m] = rotated_t[half * S:(half + 1) * S]

            @pl.when(m != sub)
            def _():
                z_copy(m, sub).start()

    z_recv[sub] = z_send[sub]

    for piece in range(8):
        turned = samples[:, piece * 128:(piece + 1) * 128].astype(F32).T.astype(BF)
        for run in range(4):
            sam_t[run % 2, piece * 64 + run // 2 * 32:piece * 64 + run // 2 * 32 + 32] = turned[
                run * 32:(run + 1) * 32
            ]
    s_copy().start()

    loads[2].wait()
    lane = lax.broadcasted_iota(jnp.int32, (KC, S), 1)

    def prepare(j, carry):
        rows = pl.ds(pl.multiple_of(j * KC, KC), KC)
        code = codes[rows, :]
        code_f = code.astype(F32)
        bias = -0.5 * jnp.sum(code_f * code_f, axis=1, keepdims=True)
        high = bias.astype(BF).astype(F32)
        rest = bias - high
        mid = rest.astype(BF).astype(F32)
        low = rest - mid
        codes_aug[rows, :S] = code
        codes_aug[rows, S:] = jnp.where(
            lane == 0, high, jnp.where(lane == 1, mid, jnp.where(lane == 2, low, 0.0))
        ).astype(BF)
        codes_ext[:S, rows] = code_f.T.astype(BF)
        codes_ext[S:, rows] = jnp.ones((16, KC), BF)
        return carry

    lax.fori_loop(0, K // KC, prepare, 0)

    ones = jnp.ones((S, ROWS), BF)
    low_start = jnp.full((8, ROWS), -jnp.inf, F32)
    acc_start = jnp.zeros((EXT, ROWS), F32)
    logits = (logits_a, logits_b)
    row16 = lax.broadcasted_iota(jnp.int32, (16, ROWS), 0)

    def first(z_aug, j, out, top):
        rows = pl.ds(j * KC, KC)
        value = jnp.dot(codes_aug[rows, :], z_aug, preferred_element_type=F32)
        out[rows, :] = value
        return jnp.maximum(top, jnp.max(value.reshape(KC // 8, 8, ROWS), axis=0))

    def second(cols, j, src, top, acc):
        rows = pl.ds(j * KC, KC)
        w = jnp.exp2(src[rows, :] * SCALE - top).astype(BF)
        weights[rows, cols] = w
        return acc + jnp.dot(codes_ext[:, rows], w, preferred_element_type=F32)

    def finish(t, cols, acc):
        who = owner(t)
        inverse = 1.0 / acc[S:S + 1]
        rebuilt = (acc[:S] * inverse).astype(BF)
        zl[:S, cols] = (z_recv[who].astype(F32) * inverse).astype(BF)
        high = inverse.astype(BF).astype(F32)
        zl[S:, cols] = jnp.where(row16 == 0, high, jnp.where(row16 == 1, inverse - high, 0.0)).astype(BF)
        return who, rebuilt

    def forward(t):
        m = origin(t)

        @pl.when(t != 0)
        def _():
            r_copy(sub, m).wait_recv()

        f_copy(m).start()

    def cross(t):
        m = origin(t)
        f_copy(m).wait_recv()
        part = lax.dot_general(sam_t[core], reb_recv[m], NT, preferred_element_type=F32)
        part = part + lax.dot_general(sam_sib[...], reb_sib[m], NT, preferred_element_type=F32)

        @pl.when(t == 0)
        def _():
            cov_own[...] = part

        @pl.when(t != 0)
        def _():
            cov_send[m] = part.astype(BF)
            c_copy(m, sub).start()

    z0 = jnp.concatenate([z_recv[sub], ones], 0)
    top = low_start
    for j in range(K // KC):
        top = first(z0, j, logits_a, top)
    s_copy().wait_recv()

    def two_steps(tt, top):
        for half in range(2):
            t = tt * 2 + half
            cols = pl.ds(pl.multiple_of(t * ROWS, ROWS), ROWS)

            @pl.when(t < SUBS - 1)
            def _():
                z_copy(sub, owner(t + 1)).wait_recv()

            z_next = jnp.concatenate([z_recv[owner(t + 1)], ones], 0)
            level = jnp.max(top, axis=0, keepdims=True) * SCALE
            acc, top = acc_start, low_start
            for j in range(K // KC):
                acc = second(cols, j, logits[half], level, acc)
                top = first(z_next, j, logits[1 - half], top)
            who, rebuilt = finish(t, cols, acc)

            @pl.when(t == 0)
            def _():
                reb_recv[sub] = rebuilt

            @pl.when(t != 0)
            def _():
                reb_send[who] = rebuilt
                r_copy(who, sub).start()

            @pl.when(tt >= 1)
            def _():
                forward(t - 2)

            @pl.when(tt >= 2)
            def _():
                cross(t - 4)

        return top

    lax.fori_loop(0, SUBS // 2, two_steps, top)

    def sums(j):
        g = (chip // 2 + 1 + j) % 8
        value = lax.dot_general(
            weights[pl.ds(pl.multiple_of(g * TC, TC), TC), :], zl[...], NT, preferred_element_type=F32
        )
        for h in range(2):
            for p in range(2):
                block = value[(h * 2 + p) * 128:(h * 2 + p + 1) * 128]
                counts = block[:, S:].T
                tot_f[g, p, h, :S] = block[:, :S]
                tot_f[g, p, h, S:] = counts
                tot_b[g, p, h, :S] = block[:, :S].astype(BF)
                tot_b[g, p, h, S:] = counts.astype(BF)
        ts_copy(g).start()

    def share(j):
        g = (chip // 2 + 1 + j) % 8
        ts_copy(g).wait_recv()
        for h in range(2):
            q = g * 2 + h
            both = tot_f[g, core, h] + tot_sib[g, h].astype(F32)

            @pl.when(q == chip)
            def _():
                tot_own[...] = both

            @pl.when(q != chip)
            def _():
                tot_send[q] = both.astype(BF)
                t_copy(q, chip).start()

    def sums_step(j, carry):
        sums(j)

        @pl.when(j >= 2)
        def _():
            share(j - 2)

        @pl.when(j < 2)
        def _():
            forward(6 + j)

        @pl.when(j < 4)
        def _():
            cross(4 + j)

        return carry

    lax.fori_loop(0, 8, sums_step, 0)
    share(6)
    share(7)

    def gather_cov(j, carry):
        src = (sub + j) % SUBS
        c_copy(sub, src).wait_recv()
        cov_own[...] = cov_own[...] + cov_recv[src].astype(F32)
        return carry

    lax.fori_loop(1, SUBS, gather_cov, 0)

    def spread_cov(j, carry):
        q = (chip + j) % CHIPS
        cov2_send[q] = cov_own[pl.ds(pl.multiple_of(q * 32, 32), 32), :].astype(BF)
        c2_copy(q, chip).start()
        return carry

    lax.fori_loop(1, CHIPS, spread_cov, 0)

    def gather_tot(j, acc):
        src = (chip + j) % CHIPS
        t_copy(chip, src).wait_recv()
        return acc + tot_recv[src].astype(F32)

    total = lax.fori_loop(1, CHIPS, gather_tot, tot_own[...])
    count = jnp.broadcast_to(total[S:S + 1] + total[S + 1:S + 2] + 1.0, (128, 128)).T
    mine = codes[pl.ds(pl.multiple_of(item * 128, 128), 128), :].astype(F32)
    fresh_ref[0] = (total[:S] + mine) / count

    def gather_cov2(j, acc):
        src = (chip + j) % CHIPS
        c2_copy(chip, src).wait_recv()
        return acc + cov2_recv[src].astype(F32)

    cross_ref[...] = lax.fori_loop(
        1, CHIPS, gather_cov2, cov_own[pl.ds(pl.multiple_of(chip * 32, 32), 32), :]
    )

    def sent_sub(j, carry):
        other = (sub + j) % SUBS
        z_copy(other, sub).wait_send()
        r_copy(other, sub).wait_send()
        c_copy(other, sub).wait_send()
        return carry

    def sent_all(j, carry):
        f_copy(j).wait_send()
        ts_copy(j).wait_send()
        return carry

    def sent_chip(j, carry):
        other = (chip + j) % CHIPS
        t_copy(other, chip).wait_send()
        c2_copy(other, chip).wait_send()
        return carry

    lax.fori_loop(1, SUBS, sent_sub, 0)
    lax.fori_loop(0, SUBS, sent_all, 0)
    lax.fori_loop(1, CHIPS, sent_chip, 0)
    s_copy().wait_send()


def body(samples, rotation, codebook):
    dma = pltpu.SemaphoreType.DMA
    return pl.pallas_call(
        kernel,
        out_shape=(
            jax.ShapeDtypeStruct((1, 128, S), F32),
            jax.ShapeDtypeStruct((32, 128), F32),
        ),
        in_specs=[pl.BlockSpec(memory_space=pl.ANY)] * 3,
        out_specs=[pl.BlockSpec(memory_space=pltpu.VMEM)] * 2,
        scratch_shapes=[
            pltpu.VMEM((ROWS, D), BF),
            pltpu.VMEM((D, D), BF),
            pltpu.VMEM((K, S), BF),
            pltpu.VMEM((K, 2 * S), BF),
            pltpu.VMEM((EXT, K), BF),
            pltpu.VMEM((2, D // 2, ROWS), BF),
            pltpu.VMEM((D // 2, ROWS), BF),
            pltpu.VMEM((SUBS, S, ROWS), BF),
            pltpu.VMEM((SUBS, S, ROWS), BF),
            pltpu.VMEM((EXT, SUBS * ROWS), BF),
            pltpu.VMEM((K, ROWS), F32),
            pltpu.VMEM((K, ROWS), F32),
            pltpu.VMEM((K, SUBS * ROWS), BF),
            pltpu.VMEM((SUBS, S, ROWS), BF),
            pltpu.VMEM((SUBS, S, ROWS), BF),
            pltpu.VMEM((SUBS, S, ROWS), BF),
            pltpu.VMEM((D // 2, S), F32),
            pltpu.VMEM((SUBS, D // 2, S), BF),
            pltpu.VMEM((SUBS, D // 2, S), BF),
            pltpu.VMEM((32, S), F32),
            pltpu.VMEM((CHIPS, 32, S), BF),
            pltpu.VMEM((CHIPS, 32, S), BF),
            pltpu.VMEM((8, 2, 2, EXT, S), F32),
            pltpu.VMEM((8, 2, 2, EXT, S), BF),
            pltpu.VMEM((8, 2, EXT, S), BF),
            pltpu.VMEM((EXT, S), F32),
            pltpu.VMEM((CHIPS, EXT, S), BF),
            pltpu.VMEM((CHIPS, EXT, S), BF),
            dma((3,)),
            dma((SUBS,)), dma((SUBS,)),
            dma((SUBS,)), dma((SUBS,)),
            dma((SUBS,)), dma((SUBS,)),
            dma, dma,
            dma((SUBS,)), dma((SUBS,)),
            dma((CHIPS,)), dma((CHIPS,)),
            dma((8,)), dma((8,)),
            dma((CHIPS,)), dma((CHIPS,)),
        ],
        compiler_params=pltpu.CompilerParams(
            collective_id=0, has_side_effects=True, vmem_limit_bytes=58 * 2**20
        ),
        cost_estimate=pl.CostEstimate(
            flops=8 * 10**9, bytes_accessed=4 * 2**20, transcendentals=K * SUBS * ROWS
        ),
        name="quantize",
    )(samples, rotation, codebook)


def solution(mesh):
    return jax.shard_map(
        body,
        mesh=mesh,
        in_specs=(P(("item", "sub"), None), P(), P("sub", None, None)),
        out_specs=(P("sub", "item", None), P("item", "sub")),
        check_vma=False,
    )
```

```python
import math

import jax
import jax.numpy as jnp
from jax import lax
from jax.experimental import pallas as pl
from jax.experimental.pallas import tpu as pltpu
from jax.sharding import PartitionSpec as P

BF = jnp.bfloat16
F32 = jnp.float32
MESH = pl.DeviceIdType.MESH
NT = (((1,), (1,)), ((), ()))

D, S, K, ROWS, SUBS = 1024, 128, 4096, 256, 8
KC = 512
TC = 512
LAG_F, LAG_C = 3, 5
EXT = S + 16
SCALE = 3.0 / math.sqrt(S) * math.log2(math.e)


def kernel(
    samples_hbm, rotation_hbm, codebook_hbm,
    fresh_ref, cross_ref,
    samples, rotation, codes, codes_aug, codes_ext,
    sam_t, sam_sib,
    z_send, z_recv, zl, logits_a, logits_b, weights,
    reb_send, reb_recv, reb_sib,
    cov_send, a_own, a_recv, b_own, b_recv, a2_own, a2_send, a2_recv, b2_own, b2_send, b2_recv,
    fin, c3_send, c3_recv,
    tot_f, tot_b, tot_sib, tot_own, tot_x, x_recv, tot_send, tot_recv,
    load_sem, z_ss, z_rs, r_ss, r_rs, f_ss, f_rs, s_ss, s_rs,
    a_ss, a_rs, b_ss, b_rs, a2_ss, a2_rs, b2_ss, b2_rs, c3_ss, c3_rs,
    ts_ss, ts_rs, tx_ss, tx_rs, t_ss, t_rs,
):
    item, sub = lax.axis_index("item"), lax.axis_index("sub")
    core, chip = item % 2, item // 2
    sibling = item + 1 - 2 * core
    xl, y = sub // 4, sub % 4
    xh, z = chip // 8, chip % 8
    x = xh * 2 + xl

    loads = [
        pltpu.make_async_copy(samples_hbm, samples, load_sem.at[0]),
        pltpu.make_async_copy(rotation_hbm, rotation, load_sem.at[1]),
        pltpu.make_async_copy(codebook_hbm.at[0], codes, load_sem.at[2]),
    ]
    for load in loads:
        load.start()

    barrier = pltpu.get_barrier_semaphore()

    def greet(i, s):
        pl.semaphore_signal(barrier, inc=1, device_id={"item": i, "sub": s}, device_id_type=MESH)

    def greet_sub(j, carry):
        greet(item, (sub + j) % SUBS)
        return carry

    def greet_z(j, carry):
        greet((xh * 8 + (z + j) % 8) * 2 + core, sub)
        return carry

    lax.fori_loop(1, SUBS, greet_sub, 0)
    lax.fori_loop(1, 8, greet_z, 0)
    across = ((1 - xh) * 8 + z) * 2 + core
    greet(across, sub)
    greet(across, (1 - xl) * 4 + y)
    greet(sibling, sub)

    def remote(src, dst, ss, rs, i, s):
        return pltpu.make_async_remote_copy(
            src_ref=src, dst_ref=dst, send_sem=ss, recv_sem=rs,
            device_id={"item": i, "sub": s}, device_id_type=MESH,
        )

    def z_copy(dest, src):
        return remote(z_send.at[dest], z_recv.at[src], z_ss.at[dest], z_rs.at[src], item, dest)

    def r_copy(dest, src):
        return remote(reb_send.at[dest], reb_recv.at[src], r_ss.at[dest], r_rs.at[src], item, dest)

    def f_copy(m):
        return remote(reb_recv.at[m], reb_sib.at[m], f_ss.at[m], f_rs.at[m], sibling, sub)

    def s_copy():
        return remote(sam_t.at[1 - core], sam_sib, s_ss, s_rs, sibling, sub)

    def along_x(dest):
        return (dest // 2 * 8 + z) * 2 + core, dest % 2 * 4 + y

    def a_copy(dest, ym, src):
        return remote(
            cov_send.at[dest % 2 * 4 + ym, 0, dest // 2], a_recv.at[src, ym],
            a_ss.at[dest, ym], a_rs.at[src, ym], *along_x(dest),
        )

    def b_copy(dest, xm, src):
        return remote(
            cov_send.at[xm * 4 + dest, 1], b_recv.at[src, xm],
            b_ss.at[dest, xm], b_rs.at[src, xm], item, xl * 4 + dest,
        )

    def a2_copy(dest, src):
        return remote(
            a2_send.at[dest], a2_recv.at[src], a2_ss.at[dest], a2_rs.at[src], item, xl * 4 + dest
        )

    def b2_copy(dest, src):
        return remote(
            b2_send.at[dest], b2_recv.at[src], b2_ss.at[dest], b2_rs.at[src], *along_x(dest)
        )

    def c3_copy(dest, src):
        return remote(
            c3_send.at[dest], c3_recv.at[src], c3_ss.at[dest], c3_rs.at[src],
            (xh * 8 + dest) * 2 + core, sub,
        )

    def ts_copy(g):
        return remote(tot_b.at[g, 1 - core], tot_sib.at[g], ts_ss.at[g], ts_rs.at[g], sibling, sub)

    def tx_copy(zz):
        return remote(tot_x.at[zz], x_recv.at[zz], tx_ss.at[zz], tx_rs.at[zz], across, sub)

    def t_copy(dest, src):
        return remote(
            tot_send.at[dest], tot_recv.at[src], t_ss.at[dest], t_rs.at[src],
            (xh * 8 + dest) * 2 + core, sub,
        )

    def owner(t):
        return (xl + t) % 2 * 4 + (y + t // 2) % 4

    def origin(t):
        return (xl + t) % 2 * 4 + (y + 8 - t // 2) % 4

    loads[0].wait()
    loads[1].wait()

    for step in range(4):
        pair = (sub // 2 + step) % 4
        rotated = jnp.dot(
            samples[...], rotation[:, pl.ds(pl.multiple_of(pair * 256, 256), 256)],
            preferred_element_type=F32,
        )
        rotated_t = rotated.T.astype(BF)
        for half in range(2):
            m = pair * 2 + half
            z_send[m] = rotated_t[half * S:(half + 1) * S]

    pl.semaphore_wait(barrier, 7 + 7 + 2 + 1)
    for t in range(1, 4):
        z_copy(origin(t), sub).start()
    z_recv[sub] = z_send[sub]

    for piece in range(8):
        turned = samples[:, piece * 128:(piece + 1) * 128].astype(F32).T.astype(BF)
        for run in range(4):
            sam_t[run % 2, piece * 64 + run // 2 * 32:piece * 64 + run // 2 * 32 + 32] = turned[
                run * 32:(run + 1) * 32
            ]
    s_copy().start()
    for t in range(4, 6):
        z_copy(origin(t), sub).start()

    loads[2].wait()
    lane = lax.broadcasted_iota(jnp.int32, (KC, S), 1)

    def prepare(j, carry):
        rows = pl.ds(pl.multiple_of(j * KC, KC), KC)
        code = codes[rows, :]
        code_f = code.astype(F32)
        bias = -0.5 * jnp.sum(code_f * code_f, axis=1, keepdims=True)
        high = bias.astype(BF).astype(F32)
        rest = bias - high
        mid = rest.astype(BF).astype(F32)
        low = rest - mid
        codes_aug[rows, :S] = code
        codes_aug[rows, S:] = jnp.where(
            lane == 0, high, jnp.where(lane == 1, mid, jnp.where(lane == 2, low, 0.0))
        ).astype(BF)
        codes_ext[:S, rows] = code_f.T.astype(BF)
        codes_ext[S:, rows] = jnp.ones((16, KC), BF)
        return carry

    lax.fori_loop(0, K // KC // 2, prepare, 0)
    for t in range(6, SUBS):
        z_copy(origin(t), sub).start()
    lax.fori_loop(K // KC // 2, K // KC, prepare, 0)

    ones = jnp.ones((S, ROWS), BF)
    low_start = jnp.full((8, ROWS), -jnp.inf, F32)
    acc_start = jnp.zeros((EXT, ROWS), F32)
    logits = (logits_a, logits_b)
    row16 = lax.broadcasted_iota(jnp.int32, (16, ROWS), 0)

    def first(z_aug, j, out, top):
        rows = pl.ds(j * KC, KC)
        value = jnp.dot(codes_aug[rows, :], z_aug, preferred_element_type=F32)
        out[rows, :] = value
        return jnp.maximum(top, jnp.max(value.reshape(KC // 8, 8, ROWS), axis=0))

    def second(cols, j, src, top, acc):
        rows = pl.ds(j * KC, KC)
        w = jnp.exp2(src[rows, :] * SCALE - top).astype(BF)
        weights[rows, cols] = w
        return acc + jnp.dot(codes_ext[:, rows], w, preferred_element_type=F32)

    def finish(t, cols, acc):
        who = owner(t)
        inverse = 1.0 / acc[S:S + 1]
        rebuilt = (acc[:S] * inverse).astype(BF)
        zl[:S, cols] = (z_recv[who].astype(F32) * inverse).astype(BF)
        high = inverse.astype(BF).astype(F32)
        zl[S:, cols] = jnp.where(row16 == 0, high, jnp.where(row16 == 1, inverse - high, 0.0)).astype(BF)
        return who, rebuilt

    def forward(t):
        m = origin(t)

        @pl.when(t != 0)
        def _():
            r_copy(sub, m).wait_recv()

        f_copy(m).start()

    def cross(t):
        m = origin(t)
        f_copy(m).wait_recv()
        part = lax.dot_general(sam_t[core], reb_recv[m], NT, preferred_element_type=F32)
        part = part + lax.dot_general(sam_sib[...], reb_sib[m], NT, preferred_element_type=F32)

        xm, ym = m // 4, m % 4
        for xd in range(2):
            dest = xd * 2 + xm
            cov_send[m, 0, xd] = part[xd * 256:xd * 256 + 128].astype(BF)
            cov_send[m, 1, xd] = part[xd * 256 + 128:xd * 256 + 256].astype(BF)

            @pl.when(dest == x)
            def _():
                a_own[ym] = part[xd * 256:xd * 256 + 128]

            @pl.when(dest != x)
            def _():
                a_copy(dest, ym, x).start()

        @pl.when(ym == y)
        def _():
            for xd in range(2):
                b_own[xm * 2 + xd] = part[xd * 256 + 128:xd * 256 + 256]

        @pl.when(ym != y)
        def _():
            b_copy(ym, xm, y).start()

    def gather_a(dy):
        ym = (y + 4 - dy) % 4
        acc = a_own[ym]
        for k in range(1, 4):
            src = (x + k) % 4
            a_copy(x, ym, src).wait_recv()
            acc = acc + a_recv[src, ym].astype(F32)
        return ym, acc

    def gather_b(k):
        dest = (x + k) % 4
        xm, xd = dest % 2, dest // 2
        acc = b_own[xm * 2 + xd]
        for j in range(1, 4):
            acc = acc + b_recv[(y + j) % 4, xm, xd].astype(F32)
        return dest, acc

    def spread_a(dy):
        ym, acc = gather_a(dy)
        a2_send[ym] = acc.astype(BF)
        a2_copy(ym, y).start()

    def spread_b():
        for j in range(1, 4):
            for xm in range(2):
                b_copy(y, xm, (y + j) % 4).wait_recv()
        for k in range(1, 4):
            dest, acc = gather_b(k)
            b2_send[dest] = acc.astype(BF)
            b2_copy(dest, x).start()
        b2_own[...] = gather_b(0)[1]
        a2_own[...] = gather_a(0)[1]

    z0 = jnp.concatenate([z_recv[sub], ones], 0)
    top = low_start
    for j in range(K // KC):
        top = first(z0, j, logits_a, top)
    s_copy().wait_recv()

    def two_steps(tt, top):
        for half in range(2):
            t = tt * 2 + half
            cols = pl.ds(pl.multiple_of(t * ROWS, ROWS), ROWS)

            @pl.when(t < SUBS - 1)
            def _():
                z_copy(sub, owner(t + 1)).wait_recv()

            z_next = jnp.concatenate([z_recv[owner(t + 1)], ones], 0)
            level = jnp.max(top, axis=0, keepdims=True) * SCALE
            acc, top = acc_start, low_start
            for j in range(K // KC):
                acc = second(cols, j, logits[half], level, acc)
                top = first(z_next, j, logits[1 - half], top)
            who, rebuilt = finish(t, cols, acc)

            @pl.when(t == 0)
            def _():
                reb_recv[sub] = rebuilt

            @pl.when(t != 0)
            def _():
                reb_send[who] = rebuilt
                r_copy(who, sub).start()

            @pl.when(t >= LAG_F)
            def _():
                forward(t - LAG_F)

            @pl.when(t >= LAG_C)
            def _():
                cross(t - LAG_C)

        return top

    lax.fori_loop(0, SUBS // 2, two_steps, top)

    def group(j):
        return (xh + 1 + j // 4) % 2 * 4 + (z // 2 + 1 + j) % 4

    def sums(j):
        g = group(j)
        value = lax.dot_general(
            weights[pl.ds(pl.multiple_of(g * TC, TC), TC), :], zl[...], NT, preferred_element_type=F32
        )
        for h in range(2):
            for p in range(2):
                block = value[(h * 2 + p) * 128:(h * 2 + p + 1) * 128]
                counts = block[:, S:].T
                tot_f[g, p, h, :S] = block[:, :S]
                tot_f[g, p, h, S:] = counts
                tot_b[g, p, h, :S] = block[:, :S].astype(BF)
                tot_b[g, p, h, S:] = counts.astype(BF)
        ts_copy(g).start()

    def pair_sum(j):
        g = group(j)
        ts_copy(g).wait_recv()
        return g, [tot_f[g, core, h] + tot_sib[g, h].astype(F32) for h in range(2)]

    def share_x(j):
        g, both = pair_sum(j)
        for h in range(2):
            zz = g % 4 * 2 + h
            tot_x[zz] = both[h].astype(BF)
            tx_copy(zz).start()

    def share_z(j):
        g, both = pair_sum(j)
        for h in range(2):
            zz = g % 4 * 2 + h
            tx_copy(zz).wait_recv()
            four = both[h] + x_recv[zz].astype(F32)

            @pl.when(zz == z)
            def _():
                tot_own[...] = four

            @pl.when(zz != z)
            def _():
                tot_send[zz] = four.astype(BF)
                t_copy(zz, z).start()

    def sums_step(j, carry):
        sums(j)

        @pl.when(j < LAG_F)
        def _():
            forward(SUBS - LAG_F + j)

        @pl.when(j < LAG_C)
        def _():
            cross(SUBS - LAG_C + j)

        @pl.when((j >= 2) & (j < 6))
        def _():
            share_x(j - 2)

        @pl.when(j >= 6)
        def _():
            share_z(j - 2)

        @pl.when((j % 2 == 0) & (j >= 2))
        def _():
            spread_a(j // 2)

        return carry

    lax.fori_loop(0, 8, sums_step, 0)
    spread_b()
    share_z(6)
    share_z(7)

    acc = a2_own[...]
    for k in range(1, 4):
        a2_copy(y, (y + k) % 4).wait_recv()
        acc = acc + a2_recv[(y + k) % 4].astype(F32)
    fin[:128] = acc
    acc = b2_own[...]
    for k in range(1, 4):
        b2_copy(x, (x + k) % 4).wait_recv()
        acc = acc + b2_recv[(x + k) % 4].astype(F32)
    fin[128:] = acc

    def spread_c(j, carry):
        zz = (z + j) % 8
        c3_send[zz] = fin[pl.ds(pl.multiple_of(zz * 32, 32), 32), :].astype(BF)
        c3_copy(zz, z).start()
        return carry

    lax.fori_loop(1, 8, spread_c, 0)

    def gather_tot(j, acc):
        src = (z + j) % 8
        t_copy(z, src).wait_recv()
        return acc + tot_recv[src].astype(F32)

    total = lax.fori_loop(1, 8, gather_tot, tot_own[...])
    count = jnp.broadcast_to(total[S:S + 1] + total[S + 1:S + 2] + 1.0, (128, 128)).T
    mine = codes[pl.ds(pl.multiple_of(item * 128, 128), 128), :].astype(F32)
    fresh_ref[0] = (total[:S] + mine) / count

    def gather_c(j, acc):
        src = (z + j) % 8
        c3_copy(z, src).wait_recv()
        return acc + c3_recv[src].astype(F32)

    cross_ref[...] = lax.fori_loop(1, 8, gather_c, fin[pl.ds(pl.multiple_of(z * 32, 32), 32), :])

    def sent_sub(j, carry):
        other = (sub + j) % SUBS
        z_copy(other, sub).wait_send()
        r_copy(other, sub).wait_send()
        return carry

    def sent_all(j, carry):
        f_copy(j).wait_send()
        ts_copy(j).wait_send()
        tx_copy(j).wait_send()
        return carry

    def sent_z(j, carry):
        other = (z + j) % 8
        t_copy(other, z).wait_send()
        c3_copy(other, z).wait_send()
        return carry

    def sent_ring(j, carry):
        for ym in range(4):
            a_copy((x + j) % 4, ym, x).wait_send()
        for xm in range(2):
            b_copy((y + j) % 4, xm, y).wait_send()
        a2_copy((y + j) % 4, y).wait_send()
        b2_copy((x + j) % 4, x).wait_send()
        return carry

    lax.fori_loop(1, SUBS, sent_sub, 0)
    lax.fori_loop(0, SUBS, sent_all, 0)
    lax.fori_loop(1, 8, sent_z, 0)
    lax.fori_loop(1, 4, sent_ring, 0)
    s_copy().wait_send()


def body(samples, rotation, codebook):
    dma = pltpu.SemaphoreType.DMA
    return pl.pallas_call(
        kernel,
        out_shape=(
            jax.ShapeDtypeStruct((1, 128, S), F32),
            jax.ShapeDtypeStruct((32, 128), F32),
        ),
        in_specs=[pl.BlockSpec(memory_space=pl.ANY)] * 3,
        out_specs=[pl.BlockSpec(memory_space=pltpu.VMEM)] * 2,
        scratch_shapes=[
            pltpu.VMEM((ROWS, D), BF),
            pltpu.VMEM((D, D), BF),
            pltpu.VMEM((K, S), BF),
            pltpu.VMEM((K, 2 * S), BF),
            pltpu.VMEM((EXT, K), BF),
            pltpu.VMEM((2, D // 2, ROWS), BF),
            pltpu.VMEM((D // 2, ROWS), BF),
            pltpu.VMEM((SUBS, S, ROWS), BF),
            pltpu.VMEM((SUBS, S, ROWS), BF),
            pltpu.VMEM((EXT, SUBS * ROWS), BF),
            pltpu.VMEM((K, ROWS), F32),
            pltpu.VMEM((K, ROWS), F32),
            pltpu.VMEM((K, SUBS * ROWS), BF),
            pltpu.VMEM((SUBS, S, ROWS), BF),
            pltpu.VMEM((SUBS, S, ROWS), BF),
            pltpu.VMEM((SUBS, S, ROWS), BF),
            pltpu.VMEM((SUBS, 2, 2, 128, S), BF),
            pltpu.VMEM((4, 128, S), F32),
            pltpu.VMEM((4, 4, 128, S), BF),
            pltpu.VMEM((4, 128, S), F32),
            pltpu.VMEM((4, 2, 2, 128, S), BF),
            pltpu.VMEM((128, S), F32),
            pltpu.VMEM((4, 128, S), BF),
            pltpu.VMEM((4, 128, S), BF),
            pltpu.VMEM((128, S), F32),
            pltpu.VMEM((4, 128, S), BF),
            pltpu.VMEM((4, 128, S), BF),
            pltpu.VMEM((256, S), F32),
            pltpu.VMEM((8, 32, S), BF),
            pltpu.VMEM((8, 32, S), BF),
            pltpu.VMEM((8, 2, 2, EXT, S), F32),
            pltpu.VMEM((8, 2, 2, EXT, S), BF),
            pltpu.VMEM((8, 2, EXT, S), BF),
            pltpu.VMEM((EXT, S), F32),
            pltpu.VMEM((8, EXT, S), BF),
            pltpu.VMEM((8, EXT, S), BF),
            pltpu.VMEM((8, EXT, S), BF),
            pltpu.VMEM((8, EXT, S), BF),
            dma((3,)),
            dma((SUBS,)), dma((SUBS,)),
            dma((SUBS,)), dma((SUBS,)),
            dma((SUBS,)), dma((SUBS,)),
            dma, dma,
            dma((4, 4)), dma((4, 4)),
            dma((4, 2)), dma((4, 2)),
            dma((4,)), dma((4,)),
            dma((4,)), dma((4,)),
            dma((8,)), dma((8,)),
            dma((8,)), dma((8,)),
            dma((8,)), dma((8,)),
            dma((8,)), dma((8,)),
        ],
        compiler_params=pltpu.CompilerParams(
            collective_id=0, has_side_effects=True, vmem_limit_bytes=58 * 2**20
        ),
        cost_estimate=pl.CostEstimate(
            flops=8 * 10**9, bytes_accessed=4 * 2**20, transcendentals=K * SUBS * ROWS
        ),
        name="quantize",
    )(samples, rotation, codebook)


def solution(mesh):
    return jax.shard_map(
        body,
        mesh=mesh,
        in_specs=(P(("item", "sub"), None), P(), P("sub", None, None)),
        out_specs=(P("sub", "item", None), P("item", "sub")),
        check_vma=False,
    )
```

```python
import math

import jax
import jax.numpy as jnp
from jax import lax
from jax.experimental import pallas as pl
from jax.experimental.pallas import tpu as pltpu
from jax.sharding import PartitionSpec as P

BF = jnp.bfloat16
F32 = jnp.float32
MESH = pl.DeviceIdType.MESH
NT = (((1,), (1,)), ((), ()))

D, S, K, ROWS, SUBS = 1024, 128, 4096, 256, 8
KC = 512
TC = 512
LAG_F, LAG_C = 4, 6
FORWARDS = {0: (4,), 1: (5,), 2: (6, 7)}
CROSSES = {0: (2,), 1: (3,), 2: (4,), 3: (5,), 4: (6, 7)}
SPREADS = {5: (1,), 6: (2,), 7: (3,)}
SPREAD_B = 8
EXT = S + 16
SCALE = 3.0 / math.sqrt(S) * math.log2(math.e)


def kernel(
    samples_hbm, rotation_hbm, codebook_hbm,
    fresh_ref, cross_ref,
    samples, rotation, codes, codes_aug, codes_ext,
    sam_t, sam_sib,
    z_send, z_recv, zl, logits_a, logits_b, weights,
    reb_send, reb_recv, reb_sib,
    cov_send, a_own, a_recv, b_own, b_recv, a2_own, a2_send, a2_recv, b2_own, b2_send, b2_recv,
    fin, c3_send, c3_recv,
    tot_b, tot_sib, tot_own, tot_x, x_recv, tot_send, tot_recv,
    load_sem, z_ss, z_rs, r_ss, r_rs, f_ss, f_rs, s_ss, s_rs,
    a_ss, a_rs, b_ss, b_rs, a2_ss, a2_rs, b2_ss, b2_rs, c3_ss, c3_rs,
    ts_ss, ts_rs, tx_ss, tx_rs, t_ss, t_rs,
):
    item, sub = lax.axis_index("item"), lax.axis_index("sub")
    core, chip = item % 2, item // 2
    sibling = item + 1 - 2 * core
    xl, y = sub // 4, sub % 4
    xh, z = chip // 8, chip % 8
    x = xh * 2 + xl

    loads = [
        pltpu.make_async_copy(samples_hbm, samples, load_sem.at[0]),
        pltpu.make_async_copy(rotation_hbm, rotation, load_sem.at[1]),
        pltpu.make_async_copy(codebook_hbm.at[0], codes, load_sem.at[2]),
    ]
    for load in loads:
        load.start()

    barrier = pltpu.get_barrier_semaphore()

    def greet(i, s):
        pl.semaphore_signal(barrier, inc=1, device_id={"item": i, "sub": s}, device_id_type=MESH)

    def greet_sub(j, carry):
        greet(item, (sub + j) % SUBS)
        return carry

    def greet_z(j, carry):
        greet((xh * 8 + (z + j) % 8) * 2 + core, sub)
        return carry

    lax.fori_loop(1, SUBS, greet_sub, 0)
    lax.fori_loop(1, 8, greet_z, 0)
    across = ((1 - xh) * 8 + z) * 2 + core
    greet(across, sub)
    greet(across, (1 - xl) * 4 + y)
    greet(sibling, sub)

    def remote(src, dst, ss, rs, i, s):
        return pltpu.make_async_remote_copy(
            src_ref=src, dst_ref=dst, send_sem=ss, recv_sem=rs,
            device_id={"item": i, "sub": s}, device_id_type=MESH,
        )

    def z_copy(dest, src):
        return remote(z_send.at[dest], z_recv.at[src], z_ss.at[dest], z_rs.at[src], item, dest)

    def r_copy(dest, src):
        return remote(reb_send.at[dest], reb_recv.at[src], r_ss.at[dest], r_rs.at[src], item, dest)

    def f_copy(m):
        return remote(reb_recv.at[m], reb_sib.at[m], f_ss.at[m], f_rs.at[m], sibling, sub)

    def s_copy():
        return remote(sam_t.at[1 - core], sam_sib, s_ss, s_rs, sibling, sub)

    def along_x(dest):
        return (dest // 2 * 8 + z) * 2 + core, dest % 2 * 4 + y

    def a_copy(dest, ym, src):
        return remote(
            cov_send.at[dest % 2 * 4 + ym, 0, dest // 2], a_recv.at[src, ym],
            a_ss.at[dest, ym], a_rs.at[src, ym], *along_x(dest),
        )

    def b_copy(dest, xm, src):
        return remote(
            cov_send.at[xm * 4 + dest, 1], b_recv.at[src, xm],
            b_ss.at[dest, xm], b_rs.at[src, xm], item, xl * 4 + dest,
        )

    def a2_copy(dest, src):
        return remote(
            a2_send.at[dest], a2_recv.at[src], a2_ss.at[dest], a2_rs.at[src], item, xl * 4 + dest
        )

    def b2_copy(dest, src):
        return remote(
            b2_send.at[dest], b2_recv.at[src], b2_ss.at[dest], b2_rs.at[src], *along_x(dest)
        )

    def c3_copy(dest, src):
        return remote(
            c3_send.at[dest], c3_recv.at[src], c3_ss.at[dest], c3_rs.at[src],
            (xh * 8 + dest) * 2 + core, sub,
        )

    def ts_copy(g):
        return remote(tot_b.at[g], tot_sib.at[g], ts_ss.at[g], ts_rs.at[g], sibling, sub)

    def tx_copy(zz):
        return remote(tot_x.at[zz], x_recv.at[zz], tx_ss.at[zz], tx_rs.at[zz], across, sub)

    def t_copy(dest, src):
        return remote(
            tot_send.at[dest], tot_recv.at[src], t_ss.at[dest], t_rs.at[src],
            (xh * 8 + dest) * 2 + core, sub,
        )

    def owner(t):
        return (xl + t + 1) % 2 * 4 + (y + (t + 1) // 2) % 4

    def origin(t):
        return (xl + t + 1) % 2 * 4 + (y + 8 - (t + 1) // 2) % 4

    loads[0].wait()
    loads[1].wait()

    for step in range(4):
        pair = (sub // 2 + step) % 4
        rotated = jnp.dot(
            samples[...], rotation[:, pl.ds(pl.multiple_of(pair * 256, 256), 256)],
            preferred_element_type=F32,
        )
        rotated_t = rotated.T.astype(BF)
        for half in range(2):
            m = pair * 2 + half
            z_send[m] = rotated_t[half * S:(half + 1) * S]

    pl.semaphore_wait(barrier, 7 + 7 + 2 + 1)
    for t in range(3):
        z_copy(origin(t), sub).start()
    z_recv[sub] = z_send[sub]

    for piece in range(8):
        turned = samples[:, piece * 128:(piece + 1) * 128].astype(F32).T.astype(BF)
        for run in range(4):
            sam_t[run % 2, piece * 64 + run // 2 * 32:piece * 64 + run // 2 * 32 + 32] = turned[
                run * 32:(run + 1) * 32
            ]
    s_copy().start()
    for t in range(3, 5):
        z_copy(origin(t), sub).start()

    loads[2].wait()
    lane = lax.broadcasted_iota(jnp.int32, (KC, S), 1)

    def source(j, b):
        half = (xh + 1 + j // 4) % 2
        parity = (core + 1 + j // 2) % 2
        return pl.ds(pl.multiple_of(((half * 8 + (z + 1 + j % 2 * 4 + b) % 8) * 2 + parity) * 128, 128), 128)

    def prepare(j, carry):
        rows = pl.ds(pl.multiple_of(j * KC, KC), KC)
        code = jnp.concatenate([codes[source(j, b), :] for b in range(4)], 0)
        code_f = code.astype(F32)
        bias = -0.5 * jnp.sum(code_f * code_f, axis=1, keepdims=True)
        high = bias.astype(BF).astype(F32)
        rest = bias - high
        mid = rest.astype(BF).astype(F32)
        low = rest - mid
        codes_aug[rows, :S] = code
        codes_aug[rows, S:] = jnp.where(
            lane == 0, high, jnp.where(lane == 1, mid, jnp.where(lane == 2, low, 0.0))
        ).astype(BF)
        codes_ext[:S, rows] = code_f.T.astype(BF)
        codes_ext[S:, rows] = jnp.ones((16, KC), BF)
        return carry

    lax.fori_loop(0, K // KC // 2, prepare, 0)
    for t in range(5, SUBS - 1):
        z_copy(origin(t), sub).start()
    lax.fori_loop(K // KC // 2, K // KC, prepare, 0)

    ones = jnp.ones((S, ROWS), BF)
    low_start = jnp.full((8, ROWS), -jnp.inf, F32)
    acc_start = jnp.zeros((EXT, ROWS), F32)
    logits = (logits_a, logits_b)
    row16 = lax.broadcasted_iota(jnp.int32, (16, ROWS), 0)

    def first(z_aug, j, out, top):
        rows = pl.ds(j * KC, KC)
        value = jnp.dot(codes_aug[rows, :], z_aug, preferred_element_type=F32)
        out[rows, :] = value
        return jnp.maximum(top, jnp.max(value.reshape(KC // 8, 8, ROWS), axis=0))

    def second(cols, j, src, top, acc):
        rows = pl.ds(j * KC, KC)
        w = jnp.exp2(src[rows, :] * SCALE - top).astype(BF)
        weights[rows, cols] = w
        return acc + jnp.dot(codes_ext[:, rows], w, preferred_element_type=F32)

    def finish(t, cols, acc):
        who = owner(t)
        inverse = 1.0 / acc[S:S + 1]
        rebuilt = (acc[:S] * inverse).astype(BF)
        zl[:S, cols] = (z_recv[who].astype(F32) * inverse).astype(BF)
        high = inverse.astype(BF).astype(F32)
        zl[S:, cols] = jnp.where(row16 == 0, high, jnp.where(row16 == 1, inverse - high, 0.0)).astype(BF)
        return who, rebuilt

    def forward(t):
        m = origin(t)

        @pl.when(t != SUBS - 1)
        def _():
            r_copy(sub, m).wait_recv()

        f_copy(m).start()

    def cross(t):
        m = origin(t)
        f_copy(m).wait_recv()
        part = lax.dot_general(sam_t[core], reb_recv[m], NT, preferred_element_type=F32)
        part = part + lax.dot_general(sam_sib[...], reb_sib[m], NT, preferred_element_type=F32)

        xm, ym = m // 4, m % 4
        for xd in range(2):
            dest = xd * 2 + xm
            cov_send[m, 0, xd] = part[xd * 256:xd * 256 + 128].astype(BF)
            cov_send[m, 1, xd] = part[xd * 256 + 128:xd * 256 + 256].astype(BF)

            @pl.when(dest == x)
            def _():
                a_own[ym] = part[xd * 256:xd * 256 + 128]

            @pl.when(dest != x)
            def _():
                a_copy(dest, ym, x).start()

        @pl.when(ym == y)
        def _():
            for xd in range(2):
                b_own[xm * 2 + xd] = part[xd * 256 + 128:xd * 256 + 256]

        @pl.when(ym != y)
        def _():
            b_copy(ym, xm, y).start()

    def gather_a(dy):
        ym = (y + 4 - dy) % 4
        acc = a_own[ym]
        for k in range(1, 4):
            src = (x + k) % 4
            a_copy(x, ym, src).wait_recv()
            acc = acc + a_recv[src, ym].astype(F32)
        return ym, acc

    def gather_b(k):
        dest = (x + k) % 4
        xm, xd = dest % 2, dest // 2
        acc = b_own[xm * 2 + xd]
        for j in range(1, 4):
            acc = acc + b_recv[(y + j) % 4, xm, xd].astype(F32)
        return dest, acc

    def spread_a(dy):
        ym, acc = gather_a(dy)
        a2_send[ym] = acc.astype(BF)
        a2_copy(ym, y).start()

    def spread_b():
        for j in range(1, 4):
            for xm in range(2):
                b_copy(y, xm, (y + j) % 4).wait_recv()
        for k in range(1, 4):
            dest, acc = gather_b(k)
            b2_send[dest] = acc.astype(BF)
            b2_copy(dest, x).start()
        b2_own[...] = gather_b(0)[1]
        a2_own[...] = gather_a(0)[1]

    z_copy(sub, owner(0)).wait_recv()
    z0 = jnp.concatenate([z_recv[owner(0)], ones], 0)
    top = low_start
    for j in range(K // KC):
        top = first(z0, j, logits_a, top)
    s_copy().wait_recv()

    def two_steps(tt, top):
        for half in range(2):
            t = tt * 2 + half
            cols = pl.ds(pl.multiple_of(t * ROWS, ROWS), ROWS)

            @pl.when(t < SUBS - 2)
            def _():
                z_copy(sub, owner(t + 1)).wait_recv()

            z_next = jnp.concatenate([z_recv[owner(t + 1)], ones], 0)
            level = jnp.max(top, axis=0, keepdims=True) * SCALE
            acc, top = acc_start, low_start
            for j in range(K // KC):
                acc = second(cols, j, logits[half], level, acc)
                top = first(z_next, j, logits[1 - half], top)
            who, rebuilt = finish(t, cols, acc)

            @pl.when(t == SUBS - 1)
            def _():
                reb_recv[sub] = rebuilt

            @pl.when(t != SUBS - 1)
            def _():
                reb_send[who] = rebuilt
                r_copy(who, sub).start()

            @pl.when(t >= LAG_F)
            def _():
                forward(t - LAG_F)

            @pl.when(t >= LAG_C)
            def _():
                cross(t - LAG_C)

        return top

    lax.fori_loop(0, SUBS // 2, two_steps, top)

    def sums(j):
        value = lax.dot_general(
            weights[j * TC:(j + 1) * TC, :], zl[...], NT, preferred_element_type=F32
        )
        return [
            jnp.concatenate([value[b * 128:b * 128 + 128, :S], value[b * 128:b * 128 + 128, S:].T], 0)
            for b in range(4)
        ]

    for j in range(8):
        pieces = sums(j)
        pair = j // 4 * 2 + j % 2
        if j // 2 % 2 == 0:
            for b in range(4):
                tot_b[pair, b] = pieces[b].astype(BF)
            ts_copy(pair).start()
        else:
            ts_copy(pair).wait_recv()
            if j >= 4:
                tx_copy(j % 2).wait_recv()
            for b in range(4):
                piece = pieces[b] + tot_sib[pair, b].astype(F32)
                if j < 4:
                    tot_x[j % 2, b] = piece.astype(BF)
                    continue
                piece = piece + x_recv[j % 2, b].astype(F32)
                if (j, b) == (7, 3):
                    tot_own[...] = piece
                else:
                    zz = (z + 1 + j % 2 * 4 + b) % 8
                    tot_send[zz] = piece.astype(BF)
                    t_copy(zz, z).start()
            if j < 4:
                tx_copy(j % 2).start()
        for step in FORWARDS.get(j, ()):
            forward(step)
        for step in CROSSES.get(j, ()):
            cross(step)
        for step in SPREADS.get(j, ()):
            spread_a(step)
        if j == SPREAD_B:
            spread_b()
    if SPREAD_B == 8:
        spread_b()

    def sent_sub(j, carry):
        other = (sub + j) % SUBS
        z_copy(other, sub).wait_send()
        r_copy(other, sub).wait_send()
        f_copy(other).wait_send()
        return carry

    def sent_ring(j, carry):
        for ym in range(4):
            a_copy((x + j) % 4, ym, x).wait_send()
        for xm in range(2):
            b_copy((y + j) % 4, xm, y).wait_send()
        return carry

    lax.fori_loop(1, SUBS, sent_sub, 0)
    f_copy(sub).wait_send()
    s_copy().wait_send()
    lax.fori_loop(1, 4, sent_ring, 0)

    acc = a2_own[...]
    for k in range(1, 4):
        a2_copy(y, (y + k) % 4).wait_recv()
        acc = acc + a2_recv[(y + k) % 4].astype(F32)
    fin[:128] = acc
    acc = b2_own[...]
    for k in range(1, 4):
        b2_copy(x, (x + k) % 4).wait_recv()
        acc = acc + b2_recv[(x + k) % 4].astype(F32)
    fin[128:] = acc

    def spread_c(j, carry):
        zz = (z + j) % 8
        c3_send[zz] = fin[pl.ds(pl.multiple_of(zz * 32, 32), 32), :].astype(BF)
        c3_copy(zz, z).start()
        return carry

    lax.fori_loop(1, 8, spread_c, 0)

    def gather_tot(j, acc):
        src = (z + j) % 8
        t_copy(z, src).wait_recv()
        return acc + tot_recv[src].astype(F32)

    total = lax.fori_loop(1, 8, gather_tot, tot_own[...])
    count = jnp.broadcast_to(total[S:S + 1] + total[S + 1:S + 2] + 1.0, (128, 128)).T
    mine = codes[pl.ds(pl.multiple_of(item * 128, 128), 128), :].astype(F32)
    fresh_ref[0] = (total[:S] + mine) / count

    def sent_z(j, carry):
        t_copy((z + j) % 8, z).wait_send()
        return carry

    def sent_c(j, carry):
        c3_copy((z + j) % 8, z).wait_send()
        return carry

    lax.fori_loop(1, 8, sent_z, 0)
    for j in range(1, 4):
        a2_copy((y + j) % 4, y).wait_send()
        b2_copy((x + j) % 4, x).wait_send()
    for j in range(4):
        ts_copy(j).wait_send()
    for j in range(2):
        tx_copy(j).wait_send()

    def gather_c(j, acc):
        src = (z + j) % 8
        c3_copy(z, src).wait_recv()
        return acc + c3_recv[src].astype(F32)

    cross_ref[...] = lax.fori_loop(1, 8, gather_c, fin[pl.ds(pl.multiple_of(z * 32, 32), 32), :])
    lax.fori_loop(1, 8, sent_c, 0)


def body(samples, rotation, codebook):
    dma = pltpu.SemaphoreType.DMA
    return pl.pallas_call(
        kernel,
        out_shape=(
            jax.ShapeDtypeStruct((1, 128, S), F32),
            jax.ShapeDtypeStruct((32, 128), F32),
        ),
        in_specs=[pl.BlockSpec(memory_space=pl.ANY)] * 3,
        out_specs=[pl.BlockSpec(memory_space=pltpu.VMEM)] * 2,
        scratch_shapes=[
            pltpu.VMEM((ROWS, D), BF),
            pltpu.VMEM((D, D), BF),
            pltpu.VMEM((K, S), BF),
            pltpu.VMEM((K, 2 * S), BF),
            pltpu.VMEM((EXT, K), BF),
            pltpu.VMEM((2, D // 2, ROWS), BF),
            pltpu.VMEM((D // 2, ROWS), BF),
            pltpu.VMEM((SUBS, S, ROWS), BF),
            pltpu.VMEM((SUBS, S, ROWS), BF),
            pltpu.VMEM((EXT, SUBS * ROWS), BF),
            pltpu.VMEM((K, ROWS), F32),
            pltpu.VMEM((K, ROWS), F32),
            pltpu.VMEM((K, SUBS * ROWS), BF),
            pltpu.VMEM((SUBS, S, ROWS), BF),
            pltpu.VMEM((SUBS, S, ROWS), BF),
            pltpu.VMEM((SUBS, S, ROWS), BF),
            pltpu.VMEM((SUBS, 2, 2, 128, S), BF),
            pltpu.VMEM((4, 128, S), F32),
            pltpu.VMEM((4, 4, 128, S), BF),
            pltpu.VMEM((4, 128, S), F32),
            pltpu.VMEM((4, 2, 2, 128, S), BF),
            pltpu.VMEM((128, S), F32),
            pltpu.VMEM((4, 128, S), BF),
            pltpu.VMEM((4, 128, S), BF),
            pltpu.VMEM((128, S), F32),
            pltpu.VMEM((4, 128, S), BF),
            pltpu.VMEM((4, 128, S), BF),
            pltpu.VMEM((256, S), F32),
            pltpu.VMEM((8, 32, S), BF),
            pltpu.VMEM((8, 32, S), BF),
            pltpu.VMEM((4, 4, EXT, S), BF),
            pltpu.VMEM((4, 4, EXT, S), BF),
            pltpu.VMEM((EXT, S), F32),
            pltpu.VMEM((2, 4, EXT, S), BF),
            pltpu.VMEM((2, 4, EXT, S), BF),
            pltpu.VMEM((8, EXT, S), BF),
            pltpu.VMEM((8, EXT, S), BF),
            dma((3,)),
            dma((SUBS,)), dma((SUBS,)),
            dma((SUBS,)), dma((SUBS,)),
            dma((SUBS,)), dma((SUBS,)),
            dma, dma,
            dma((4, 4)), dma((4, 4)),
            dma((4, 2)), dma((4, 2)),
            dma((4,)), dma((4,)),
            dma((4,)), dma((4,)),
            dma((8,)), dma((8,)),
            dma((8,)), dma((8,)),
            dma((8,)), dma((8,)),
            dma((8,)), dma((8,)),
        ],
        compiler_params=pltpu.CompilerParams(
            collective_id=0, has_side_effects=True, vmem_limit_bytes=58 * 2**20
        ),
        cost_estimate=pl.CostEstimate(
            flops=8 * 10**9, bytes_accessed=4 * 2**20, transcendentals=K * SUBS * ROWS
        ),
        name="quantize",
    )(samples, rotation, codebook)


def solution(mesh):
    return jax.shard_map(
        body,
        mesh=mesh,
        in_specs=(P(("item", "sub"), None), P(), P("sub", None, None)),
        out_specs=(P("sub", "item", None), P("item", "sub")),
        check_vma=False,
    )
```
